32 devices in a mesh: groups: 2 (over y), gx: 4 (over z), gy: 2 (over x), side: 2 (over core).
Axes of the slice: x: 2, y: 2, z: 4, core: 2. Of those that a mesh axis runs over, the one named last changes fastest.
Arguments:
- permeab: float32 [2, 64, 64, 256], P('side', None, 'gx', 'gy'), may hold values from 0.2 to 5
- diffusivity: float32 [2, 64, 64, 256], P('side', None, 'gx', 'gy'), may hold values from 0.2 to 5
- conductivity: float32 [2, 64, 64, 256], P('side', None, 'gx', 'gy'), may hold values from 0.2 to 5
- velocity: float32 [2, 64, 64, 256], P('side', None, 'gx', 'gy'), may hold values from 0.5 to 2
- overpotential: float32 [2, 64, 64, 256], P('side', None, 'gx', 'gy'), may hold values from -3 to 3
- target: float32 [2, 64, 64, 256], P('side', None, 'gx', 'gy'), may hold values from -6 to 6
- inlet_mask: int32 [2, 64, 256], P('side', 'gx', 'gy'), may hold values 0 or 1
- outlet_mask: int32 [2, 64, 256], P('side', 'gx', 'gy'), may hold values 0 or 1
- solid_mask: int32 [4, 64, 64, 256], P(('groups', 'side'), None, 'gx', 'gy'), parts along dimension 0, may hold values 0 or 1
Outputs:
- adjoints: float32 [4, 3, 64, 64, 256], P(('groups', 'side'), None, None, 'gx', 'gy'), parts along dimension 0
The draws below stay inside these ranges and needn't reach their ends.
There are 2 independent parts, one for each index of `groups`. The reference program is written for one: setup_inputs(seed, part) draws one part's arguments, and reference() takes and returns one part's arrays. A program takes and returns all parts, laid end to end along the dimension named above; an argument that names none is the same for every part. Nothing has to cross between parts.
All inputs are finite; a program needn't handle non-finite values. No bound on the sum of `inlet_mask` or of `outlet_mask` or of `solid_mask` on one device may be relied on, other than what follows from the above.
Results may differ from the reference program's by a relative error of at most 0.0001.
Values sent between devices are 32-bit elements; how exact they have to be, the bound alone decides.
A program may use at most 128 MiB of HBM per device.

```python
import math
import jax
import jax.numpy as jnp
from jax import lax

NZ = 64
ITERS = 16
NX = 64
NY = 256


def plant(result, key, smallest, largest):
    extent = result.shape
    spot = [jax.random.randint(jax.random.fold_in(key, axis), (), 0, extent[axis]) for axis in range(len(extent))]
    result = result.at[tuple(spot)].set(smallest)
    longest = extent.index(max(extent))
    spot[longest] = (spot[longest] + 1) % extent[longest]
    return result.at[tuple(spot)].set(largest)


def steps_of(stream_key, shape, shards, smallest, high):
    factor_of, own = 1.0, jax.random.fold_in(stream_key, 6)
    for dim, parts in shards:
        draws = jnp.exp(jax.random.uniform(jax.random.fold_in(own, dim), (parts,), jnp.float32, smallest / len(shards), high / len(shards)))
        factor_of = factor_of * jnp.repeat(draws, shape[dim] // parts).reshape([-1 if axis == dim else 1 for axis in range(len(shape))])
    return factor_of


def bell_draw(stream_key, shape, spread, reach, shards=(), held_as=jnp.bfloat16):
    drawn = spread * jax.random.normal(stream_key, shape, jnp.float32)
    if shards:
        drawn = drawn * steps_of(stream_key, shape, shards, -0.22, 0.18)
    return jnp.clip(drawn, -reach, reach).astype(held_as)


def setup_inputs(seed: int = 0, part: int = 0) -> dict:
    key_of = jax.random.split(jax.random.key(seed), 10)
    own_keys = jax.random.split(jax.random.fold_in(key_of[9], part), 10)
    return {
        "permeab": jnp.clip(jnp.exp(math.log(5.0) - 3.218876 * jax.random.uniform(key_of[0], (2, NZ, NX, NY), jnp.float32) ** steps_of(key_of[0], (2, NZ, NX, NY), ((0, 2), (2, 4), (3, 2)), -0.2, 0.2)), 0.2, 5.0),
        "diffusivity": jnp.clip(jnp.exp(math.log(5.0) - 3.218876 * jax.random.uniform(key_of[1], (2, NZ, NX, NY), jnp.float32) ** steps_of(key_of[1], (2, NZ, NX, NY), ((0, 2), (2, 4), (3, 2)), -0.2, 0.2)), 0.2, 5.0),
        "conductivity": jnp.clip(jnp.exp(math.log(5.0) - 3.218876 * jax.random.uniform(key_of[2], (2, NZ, NX, NY), jnp.float32) ** steps_of(key_of[2], (2, NZ, NX, NY), ((0, 2), (2, 4), (3, 2)), -0.2, 0.2)), 0.2, 5.0),
        "velocity": jnp.clip(0.5 + 1.5 * jax.random.uniform(key_of[3], (2, NZ, NX, NY), jnp.float32) ** steps_of(key_of[3], (2, NZ, NX, NY), ((0, 2), (2, 4), (3, 2)), -0.2, 0.2), 0.5, 2.0),
        "overpotential": bell_draw(key_of[4], (2, NZ, NX, NY), 0.5, 3.0, ((0, 2), (2, 4), (3, 2)), jnp.float32),
        "target": bell_draw(key_of[5], (2, NZ, NX, NY), 1.0, 6.0, ((0, 2), (2, 4), (3, 2)), jnp.float32),
        "inlet_mask": plant((jax.random.randint(key_of[6], (2, NX, NY), 0, 8) < 1).astype(jnp.int32), jax.random.fold_in(key_of[6], 1), 0, 1),
        "outlet_mask": plant((jax.random.randint(key_of[7], (2, NX, NY), 0, 8) < 1).astype(jnp.int32), jax.random.fold_in(key_of[7], 1), 0, 1),
        "solid_mask": plant((jax.random.randint(own_keys[8], (2, NZ, NX, NY), 0, 4) < 1).astype(jnp.int32), jax.random.fold_in(own_keys[8], 1), 0, 1),
    }


OMEGA = 0.8
MEMBRANE = 1.5


def adjacent_cell(arr, a, b, c):
    return arr[1 + a:arr.shape[0] - 1 + a, 1 + b:arr.shape[1] - 1 + b, 1 + c:arr.shape[2] - 1 + c]


def laplace(field_grid, coef):
    velocity_padded = jnp.pad(field_grid, ((1, 1), (0, 0), (0, 0)))
    kpad = jnp.pad(coef, ((1, 1), (0, 0), (0, 0)))
    velocity_centre = adjacent_cell(velocity_padded, 0, 0, 0)
    kcen = adjacent_cell(kpad, 0, 0, 0)
    running_total = jnp.zeros(velocity_centre.shape, jnp.float32)
    dsum = jnp.zeros(velocity_centre.shape, jnp.float32)
    for index_shift in ((1, 0, 0), (-1, 0, 0), (0, 1, 0), (0, -1, 0), (0, 0, 1), (0, 0, -1)):
        stencil_weight = 0.5 * (kcen + adjacent_cell(kpad, *index_shift))
        running_total = running_total + stencil_weight * (adjacent_cell(velocity_padded, *index_shift) - velocity_centre)
        dsum = dsum + stencil_weight
    return running_total, dsum


def relax(fields, coefs, mirror):
    pres, conc, pot = fields[0], fields[1], fields[2]
    kperm, kdiff, kcond, speed, rate, inside, blocked, source = [coefs[i][:, 1:-1, 1:-1] for i in range(8)]
    lap_p, sum_p = laplace(pres, coefs[0])
    lap_c, sum_c = laplace(conc, coefs[1])
    lap_e, sum_e = laplace(pot, coefs[2])
    pcen = pres[:, 1:-1, 1:-1]
    ccen = conc[:, 1:-1, 1:-1]
    ecen = pot[:, 1:-1, 1:-1]
    ahead = conc[:, 2:, 1:-1] - ccen
    layer = (lax.broadcasted_iota(jnp.int32, pcen.shape, 0) == 0).astype(jnp.float32) * MEMBRANE
    p_new = pcen + OMEGA * (speed * ahead + lap_p - pcen) / (sum_p + 1.0)
    c_new = (ccen + OMEGA * (source + speed * ahead + lap_c - rate * (ccen - ecen)) / (sum_c + speed + rate)) * (1.0 - blocked)
    e_new = ecen + OMEGA * (lap_e + rate * (ccen - ecen) + layer * (mirror[None] - ecen)) / (sum_e + rate + layer)
    return jnp.stack([p_new, c_new, e_new]) * inside[None]


def build_coefs(permeab, diffusivity, conductivity, velocity, overpotential, target, inlet, outlet, solid, outflow, cells):
    depth = permeab.shape[0]
    top = (lax.broadcasted_iota(jnp.int32, permeab.shape, 0) == depth - 1).astype(jnp.float32)
    kperm = permeab * (1.0 - 0.95 * solid.astype(jnp.float32))
    rate = 0.5 * (jnp.exp(0.5 * overpotential) + jnp.exp(-0.5 * overpotential))
    blocked = top * inlet.astype(jnp.float32)[None]
    source = target + top * outlet.astype(jnp.float32)[None] * (cells / 8.0) / (1.0 + outflow)
    inside = jnp.ones(permeab.shape, jnp.float32)
    return jnp.stack([kperm, diffusivity, conductivity, velocity, rate, inside, blocked, source])


def reference(permeab, diffusivity, conductivity, velocity, overpotential, target, inlet_mask, outlet_mask, solid_mask):
    cells = float(NX * NY)
    coefs = []
    for side in range(2):
        outflow = jnp.sum(outlet_mask[side].astype(jnp.float32) * velocity[side, NZ - 1])
        built = build_coefs(permeab[side], diffusivity[side], conductivity[side], velocity[side], overpotential[side], target[side], inlet_mask[side], outlet_mask[side], solid_mask[side], outflow, cells)
        coefs.append(jnp.pad(built, ((0, 0), (0, 0), (1, 1), (1, 1))))
    start = jnp.zeros((2, 3, NZ, NX, NY), jnp.float32)

    def sweep(step, fields):
        news = []
        for side in range(2):
            padded = jnp.pad(fields[side], ((0, 0), (0, 0), (1, 1), (1, 1)))
            mirror = fields[1 - side, 2, 0]
            news.append(relax(padded, coefs[side], mirror))
        return jnp.stack(news)

    return lax.fori_loop(0, ITERS, sweep, start)
```

```python
import functools

import jax
import jax.numpy as jnp
from jax import lax
from jax.experimental import pallas as pl
from jax.experimental.pallas import tpu as pltpu
from jax.sharding import PartitionSpec as P

ITERS = 16
OMEGA = 0.8
MEMBRANE = 1.5
CHUNKS = 4
MESH = pl.DeviceIdType.MESH
f32 = jnp.float32


def kernel(
    ngx, ngy, depth,
    permeab, diffusivity, conductivity, velocity, overpotential, target, inlet, outlet, solid,
    out,
    F, W, sx, hx, sy, hy, keep, extra, part, got_x, got_y,
    send_sem, recv_sem, flow_send, flow_recv,
):
    zc = depth // CHUNKS
    gx, gy, side = lax.axis_index("gx"), lax.axis_index("gy"), lax.axis_index("side")
    cells = float(16 * ngx * 128 * ngy)
    lane = lax.broadcasted_iota(jnp.int32, (8, 128), 1)
    sub = lax.broadcasted_iota(jnp.int32, (8, 128), 0)
    first_lane, last_lane = lane == 0, lane == 127
    first_row, last_row = sub == 0, sub == 7
    pair = lane // 2
    even = lane % 2 == 0
    zero = jnp.zeros((8, 128), f32)

    for p in range(2):
        for f in range(3):
            F[p, f, 0] = jnp.zeros((32, 128), f32)
            F[p, f, depth + 1] = jnp.zeros((32, 128), f32)
    hx[...] = jnp.zeros(hx.shape, f32)
    hy[...] = jnp.zeros(hy.shape, f32)

    barrier = pltpu.get_barrier_semaphore()
    for d in range(1, ngx):
        pl.semaphore_signal(barrier, inc=1, device_id={"gx": lax.rem(gx + d, ngx)}, device_id_type=MESH)
    for d in range(1, ngy):
        pl.semaphore_signal(barrier, inc=1, device_id={"gy": lax.rem(gy + d, ngy)}, device_id_type=MESH)
    pl.semaphore_signal(barrier, inc=1, device_id={"side": 1 - side}, device_id_type=MESH)
    pl.semaphore_wait(barrier, ngx - 1 + ngy - 1 + 1)

    def flow_copy(axis, me, count, d, src, dst, sending):
        k = 0 if axis == "gx" else 1
        peer = lax.rem(me + d, count) if sending else lax.rem(me + count - d, count)
        slot = me if sending else peer
        return pltpu.make_async_remote_copy(
            src_ref=src, dst_ref=dst.at[slot],
            send_sem=flow_send.at[k, d], recv_sem=flow_recv.at[k, d],
            device_id={axis: peer}, device_id_type=MESH,
        )

    tile = zero
    for h in range(2):
        rows = pl.ds(8 * h, 8)
        tile = tile + outlet[0, rows].astype(f32) * velocity[0, depth - 1, rows]
    part[0] = tile
    for d in range(1, ngx):
        flow_copy("gx", gx, ngx, d, part.at[0], got_x, True).start()

    has_lower = (gx > 0, gy > 0)
    has_upper = (gx < ngx - 1, gy < ngy - 1)
    can_send = (has_upper[0], has_lower[0], has_upper[1], has_lower[1])
    can_recv = (has_lower[0], has_upper[0], has_lower[1], has_upper[1])

    def halo_copy(p, d, c):
        if d == 4:
            src, dst = F.at[p, 2, 1, pl.ds(8, 16)], F.at[p, 2, 0, pl.ds(8, 16)]
            where = {"side": 1 - side}
        elif d < 2:
            src, dst = sx.at[p, 1 - d, c], hx.at[p, d, c]
            where = {"gx": gx + 1 if d == 0 else gx - 1}
        else:
            src, dst = sy.at[p, c], hy.at[p, d - 2, c]
            where = {"gy": gy + 1 if d == 2 else gy - 1}
        return pltpu.make_async_remote_copy(
            src_ref=src, dst_ref=dst,
            send_sem=send_sem.at[p, d, c], recv_sem=recv_sem.at[p, d, c],
            device_id=where, device_id_type=MESH,
        )

    def send(p, c, membrane):
        for d in range(4):
            @pl.when(can_send[d])
            def _(d=d):
                halo_copy(p, d, c).start()
        if membrane and c == 0:
            halo_copy(p, 4, c).start()

    def receive(p, c, membrane):
        for d in range(4):
            @pl.when(can_send[d])
            def _(d=d):
                halo_copy(p, d, c).wait_send()

            @pl.when(can_recv[d])
            def _(d=d):
                halo_copy(p, d, c).wait_recv()
        if membrane and c == 0:
            copy = halo_copy(p, 4, c)
            copy.wait_send()
            copy.wait_recv()

    def columns(p, c):
        lists = []
        for f in range(3):
            upper, lower = hy[p, 1, c, f], hy[p, 0, c, f]
            lists.append(jnp.where(even, pltpu.roll(upper, 127, 1), pltpu.roll(lower, 1, 1)))
        return lists

    def around(p, c, f, iz, h, cols):
        at = c * zc + iz + 1
        r = 8 + 8 * h
        cen = F[p, f, at, pl.ds(r, 8)]
        below = F[p, f, at - 1, pl.ds(r, 8)]
        above = F[p, f, at + 1, pl.ds(r, 8)]
        xm = F[p, f, at, pl.ds(r - 1, 8)]
        xp = F[p, f, at, pl.ds(r + 1, 8)]
        if h == 0:
            xm = jnp.where(first_row, jnp.broadcast_to(hx[p, 0, c, f, pl.ds(iz, 1)], (8, 128)), xm)
        else:
            xp = jnp.where(last_row, jnp.broadcast_to(hx[p, 1, c, f, pl.ds(iz, 1)], (8, 128)), xp)
        spot = 2 * (2 * iz + h) + 1
        side_cols = pltpu.roll(cols[f], 128 - spot, 1)
        ym = jnp.where(first_lane, side_cols, pltpu.roll(cen, 1, 1))
        yp = jnp.where(last_lane, side_cols, pltpu.roll(cen, 127, 1))
        return cen, (below, above, xm, xp, ym, yp)

    def put(q, c, f, iz, h, value, packed):
        F[q, f, c * zc + iz + 1, pl.ds(8 + 8 * h, 8)] = value
        if h == 0:
            sx[q, 0, c, f, pl.ds(iz, 1)] = value[0:1]
        else:
            sx[q, 1, c, f, pl.ds(iz, 1)] = value[7:8]
        ti = 2 * iz + h
        return jnp.where(pair == ti, pltpu.roll(value, 2 * ti + 1, 1), packed)

    def chunk_of(q, c, plane, unroll, store=True):
        def body(i, packed):
            packed = list(packed)
            for u in range(unroll):
                iz = i * unroll + u
                for h in range(2):
                    values = plane(iz, h)
                    if store:
                        for f in range(3):
                            packed[f] = put(q, c, f, iz, h, values[f], packed[f])
            return tuple(packed)

        packed = lax.fori_loop(0, zc // unroll, body, (zero, zero, zero))
        if store:
            for f in range(3):
                sy[q, c, f] = packed[f]

    for c in range(CHUNKS):
        def plane(iz, h, c=c):
            z, rows = c * zc + iz, pl.ds(8 * h, 8)
            kp = permeab[0, z, rows] * (1.0 - 0.95 * solid[0, z, rows].astype(f32))
            return kp, diffusivity[0, z, rows], conductivity[0, z, rows]

        chunk_of(0, c, plane, 2)
        send(0, c, False)

    for h in range(2):
        rows = pl.ds(8 * h, 8)
        keep[0, rows] = jnp.full((8, 128), 1.0 - OMEGA, f32)
        keep[1, rows] = (1.0 - OMEGA) * (1.0 - inlet[0, rows].astype(f32))
        extra[rows] = zero

    for c in range(CHUNKS):
        if c == 0 and CHUNKS > 1:
            total = part[0]
            for d in range(1, ngx):
                flow_copy("gx", gx, ngx, d, part.at[0], got_x, True).wait_send()
                flow_copy("gx", gx, ngx, d, part.at[0], got_x, False).wait_recv()
                total = total + got_x[lax.rem(gx + ngx - d, ngx)]
            part[1] = total
            for d in range(1, ngy):
                flow_copy("gy", gy, ngy, d, part.at[1], got_y, True).start()
        if c == CHUNKS - 1:
            total = part[1]
            for d in range(1, ngy):
                flow_copy("gy", gy, ngy, d, part.at[1], got_y, True).wait_send()
                flow_copy("gy", gy, ngy, d, part.at[1], got_y, False).wait_recv()
                total = total + got_y[lax.rem(gy + ngy - d, ngy)]
            outflow = jnp.sum(jnp.sum(total, axis=0, keepdims=True), axis=1, keepdims=True)
            scale = jnp.broadcast_to((cells / 8.0) / (1.0 + outflow), (8, 128))
            for h in range(2):
                rows = pl.ds(8 * h, 8)
                extra[rows] = outlet[0, rows].astype(f32) * scale
        receive(0, c, False)
        cols = columns(0, c)

        def plane(iz, h, c=c, cols=cols):
            z, rows = c * zc + iz, pl.ds(8 * h, 8)
            bottom = (z == 0).astype(f32)
            top = (z == depth - 1).astype(f32)
            vel = velocity[0, z, rows]
            half = 0.5 * overpotential[0, z, rows]
            rate = 0.5 * (jnp.exp(half) + jnp.exp(-half))
            g = jnp.full((8, 128), MEMBRANE, f32) * bottom
            source = target[0, z, rows] + top * extra[rows]
            free = 1.0 - top * inlet[0, rows].astype(f32)
            for f, base in ((0, 0), (1, 7), (2, 15)):
                cen, near = around(0, c, f, iz, h, cols)
                w = [0.5 * (cen + k) for k in near]
                dsum = ((w[0] + w[1]) + (w[2] + w[3])) + (w[4] + w[5])
                if f == 0:
                    factor = OMEGA / (dsum + 1.0)
                    W[6, z, rows] = factor * vel
                elif f == 1:
                    factor = OMEGA * free / (dsum + vel + rate)
                    w[3] = w[3] + vel
                    start = factor * source
                    W[13, z, rows] = start
                    W[14, z, rows] = factor * rate
                else:
                    factor = OMEGA / (dsum + rate + g)
                    w[0] = w[0] * (1.0 - bottom) + g
                    W[21, z, rows] = factor * rate
                for n in range(6):
                    W[base + n, z, rows] = factor * w[n]
            return zero, start, zero

        chunk_of(1, c, plane, 2)
        send(1, c, True)

    def sweep_chunk(p, q, c, final):
        receive(p, c, True)
        cols = columns(p, c)

        def plane(iz, h):
            z, rows = c * zc + iz, pl.ds(8 * h, 8)
            top = (z == depth - 1).astype(jnp.int32)

            def mixed(base, near):
                t = [W[base + n, z, rows] * near[n] for n in range(6)]
                return ((t[0] + t[1]) + (t[2] + t[3])) + (t[4] + t[5])

            pc, pn = around(p, c, 0, iz, h, cols)
            cc, cn = around(p, c, 1, iz, h, cols)
            ec, en = around(p, c, 2, iz, h, cols)
            p_new = mixed(0, pn) + ((1.0 - OMEGA) * pc + W[6, z, rows] * (cn[3] - cc))
            c_new = mixed(7, cn) + (keep[top, rows] * cc + (W[13, z, rows] + W[14, z, rows] * ec))
            e_new = mixed(15, en) + ((1.0 - OMEGA) * ec + W[21, z, rows] * cc)
            if final:
                out[0, 0, z, rows] = p_new
                out[0, 1, z, rows] = c_new
                out[0, 2, z, rows] = e_new
            return p_new, c_new, e_new

        chunk_of(q, c, plane, 2, not final)
        if not final:
            send(q, c, True)

    def sweep(t, carry):
        p = lax.rem(t, 2)
        for c in range(CHUNKS):
            sweep_chunk(p, 1 - p, c, False)
        return carry

    lax.fori_loop(1, ITERS - 1, sweep, 0)
    last = (ITERS - 1) % 2
    for c in range(CHUNKS):
        sweep_chunk(last, 1 - last, c, True)


def solution(mesh):
    ngx, ngy = mesh.shape["gx"], mesh.shape["gy"]

    def local(*args):
        depth = args[0].shape[1]
        zc = depth // CHUNKS
        vmem = pl.BlockSpec(memory_space=pltpu.VMEM)
        return pl.pallas_call(
            functools.partial(kernel, ngx, ngy, depth),
            out_shape=jax.ShapeDtypeStruct((1, 3, depth, 16, 128), f32),
            in_specs=[vmem] * 9,
            out_specs=vmem,
            scratch_shapes=[
                pltpu.VMEM((2, 3, depth + 2, 32, 128), f32),
                pltpu.VMEM((22, depth, 16, 128), f32),
                pltpu.VMEM((2, 2, CHUNKS, 3, zc, 128), f32),
                pltpu.VMEM((2, 2, CHUNKS, 3, zc, 128), f32),
                pltpu.VMEM((2, CHUNKS, 3, 8, 128), f32),
                pltpu.VMEM((2, 2, CHUNKS, 3, 8, 128), f32),
                pltpu.VMEM((2, 16, 128), f32),
                pltpu.VMEM((16, 128), f32),
                pltpu.VMEM((2, 8, 128), f32),
                pltpu.VMEM((ngx, 8, 128), f32),
                pltpu.VMEM((ngy, 8, 128), f32),
                pltpu.SemaphoreType.DMA((2, 5, CHUNKS)),
                pltpu.SemaphoreType.DMA((2, 5, CHUNKS)),
                pltpu.SemaphoreType.DMA((2, max(ngx, ngy))),
                pltpu.SemaphoreType.DMA((2, max(ngx, ngy))),
            ],
            compiler_params=pltpu.CompilerParams(
                collective_id=0, has_side_effects=True, vmem_limit_bytes=48 * 1024 * 1024
            ),
        )(*args)

    placed = (
        (P("side", None, "gx", "gy"),) * 6
        + (P("side", "gx", "gy"),) * 2
        + (P(("groups", "side"), None, "gx", "gy"),)
    )
    return jax.shard_map(
        local,
        mesh=mesh,
        in_specs=placed,
        out_specs=P(("groups", "side"), None, None, "gx", "gy"),
        check_vma=False,
    )
```

```python
import functools

import jax
import jax.numpy as jnp
from jax import lax
from jax.experimental import pallas as pl
from jax.experimental.pallas import tpu as pltpu
from jax.sharding import PartitionSpec as P

ITERS = 16
OMEGA = 0.8
MEMBRANE = 1.5
CHUNKS = 8
UNROLL = 8
COEF_UNROLL = 4
MESH = pl.DeviceIdType.MESH
f32 = jnp.float32


def kernel(
    ngx, ngy, depth,
    permeab_hbm, diffusivity_hbm, conductivity_hbm, velocity_hbm, overpotential_hbm,
    target_hbm, inlet_hbm, outlet_hbm, solid_hbm,
    out_hbm,
    permeab, diffusivity, conductivity, velocity, overpotential, target, inlet, outlet, solid, out,
    F, W, sx, hx, sy, hy, keep, extra, part, got_x, got_y,
    send_sem, recv_sem, flow_send, flow_recv, in_sem, out_sem,
):
    loads = [
        pltpu.make_async_copy(src, dst, in_sem.at[n])
        for n, (src, dst) in enumerate(
            (
                (outlet_hbm, outlet), (inlet_hbm, inlet), (solid_hbm, solid),
                (permeab_hbm, permeab), (diffusivity_hbm, diffusivity),
                (conductivity_hbm, conductivity), (velocity_hbm, velocity),
                (overpotential_hbm, overpotential), (target_hbm, target),
            )
        )
    ]
    for load in loads:
        load.start()
    zc = depth // CHUNKS
    gx, gy, side = lax.axis_index("gx"), lax.axis_index("gy"), lax.axis_index("side")
    cells = float(16 * ngx * 128 * ngy)
    lane = lax.broadcasted_iota(jnp.int32, (8, 128), 1)
    sub = lax.broadcasted_iota(jnp.int32, (8, 128), 0)
    first_lane, last_lane = lane == 0, lane == 127
    first_row, last_row = sub == 0, sub == 7
    pair = lane // 2
    even = lane % 2 == 0
    zero = jnp.zeros((8, 128), f32)

    for p in range(2):
        for f in range(3):
            F[p, f, 0] = jnp.zeros((32, 128), f32)
            F[p, f, depth + 1] = jnp.zeros((32, 128), f32)
    hx[...] = jnp.zeros(hx.shape, f32)
    hy[...] = jnp.zeros(hy.shape, f32)

    barrier = pltpu.get_barrier_semaphore()
    for d in range(1, ngx):
        pl.semaphore_signal(barrier, inc=1, device_id={"gx": lax.rem(gx + d, ngx)}, device_id_type=MESH)
    for d in range(1, ngy):
        pl.semaphore_signal(barrier, inc=1, device_id={"gy": lax.rem(gy + d, ngy)}, device_id_type=MESH)
    pl.semaphore_signal(barrier, inc=1, device_id={"side": 1 - side}, device_id_type=MESH)
    pl.semaphore_wait(barrier, ngx - 1 + ngy - 1 + 1)

    def flow_copy(axis, me, count, d, src, dst, sending):
        k = 0 if axis == "gx" else 1
        peer = lax.rem(me + d, count) if sending else lax.rem(me + count - d, count)
        slot = me if sending else peer
        return pltpu.make_async_remote_copy(
            src_ref=src, dst_ref=dst.at[slot],
            send_sem=flow_send.at[k, d], recv_sem=flow_recv.at[k, d],
            device_id={axis: peer}, device_id_type=MESH,
        )

    has_lower = (gx > 0, gy > 0)
    has_upper = (gx < ngx - 1, gy < ngy - 1)
    can_send = (has_upper[0], has_lower[0], has_upper[1], has_lower[1])
    can_recv = (has_lower[0], has_upper[0], has_lower[1], has_upper[1])

    def halo_copy(p, d, c):
        if d == 4:
            src, dst = F.at[p, 2, 1, pl.ds(8, 16)], F.at[p, 2, 0, pl.ds(8, 16)]
            where = {"side": 1 - side}
        elif d < 2:
            src, dst = sx.at[p, 1 - d, c], hx.at[p, d, c]
            where = {"gx": gx + 1 if d == 0 else gx - 1}
        else:
            src, dst = sy.at[p, c], hy.at[p, d - 2, c]
            where = {"gy": gy + 1 if d == 2 else gy - 1}
        return pltpu.make_async_remote_copy(
            src_ref=src, dst_ref=dst,
            send_sem=send_sem.at[p, d, c], recv_sem=recv_sem.at[p, d, c],
            device_id=where, device_id_type=MESH,
        )

    def send(p, c, membrane):
        for d in range(4):
            @pl.when(can_send[d])
            def _(d=d):
                halo_copy(p, d, c).start()
        if membrane:
            @pl.when(c == 0)
            def _():
                halo_copy(p, 4, 0).start()

    def receive(p, c, membrane):
        for d in range(4):
            @pl.when(can_send[d])
            def _(d=d):
                halo_copy(p, d, c).wait_send()

            @pl.when(can_recv[d])
            def _(d=d):
                halo_copy(p, d, c).wait_recv()
        if membrane:
            @pl.when(c == 0)
            def _():
                copy = halo_copy(p, 4, 0)
                copy.wait_send()
                copy.wait_recv()

    def columns(p, c):
        lists = []
        for f in range(3):
            upper, lower = hy[p, 1, c, f], hy[p, 0, c, f]
            lists.append(jnp.where(even, pltpu.roll(upper, 127, 1), pltpu.roll(lower, 1, 1)))
        return lists

    def around(p, c, f, iz, h, cols):
        at = c * zc + iz + 1
        r = 8 + 8 * h
        cen = F[p, f, at, pl.ds(r, 8)]
        below = F[p, f, at - 1, pl.ds(r, 8)]
        above = F[p, f, at + 1, pl.ds(r, 8)]
        xm = F[p, f, at, pl.ds(r - 1, 8)]
        xp = F[p, f, at, pl.ds(r + 1, 8)]
        if h == 0:
            xm = jnp.where(first_row, jnp.broadcast_to(hx[p, 0, c, f, pl.ds(iz, 1)], (8, 128)), xm)
        else:
            xp = jnp.where(last_row, jnp.broadcast_to(hx[p, 1, c, f, pl.ds(iz, 1)], (8, 128)), xp)
        spot = 2 * (2 * iz + h) + 1
        side_cols = pltpu.roll(cols[f], 128 - spot, 1)
        ym = jnp.where(first_lane, side_cols, pltpu.roll(cen, 1, 1))
        yp = jnp.where(last_lane, side_cols, pltpu.roll(cen, 127, 1))
        return cen, (below, above, xm, xp, ym, yp)

    def put(q, c, f, iz, h, value, packed):
        F[q, f, c * zc + iz + 1, pl.ds(8 + 8 * h, 8)] = value
        if h == 0:
            sx[q, 0, c, f, pl.ds(iz, 1)] = value[0:1]
        else:
            sx[q, 1, c, f, pl.ds(iz, 1)] = value[7:8]
        ti = 2 * iz + h
        return jnp.where(pair == ti, pltpu.roll(value, 2 * ti + 1, 1), packed)

    def chunk_of(q, c, plane, unroll, store=True):
        def body(i, packed):
            packed = list(packed)
            spots = [(i * unroll + u, h) for u in range(unroll) for h in range(2)]
            tiles = [plane(iz, h) for iz, h in spots]
            for (iz, h), values in zip(spots, tiles):
                for n, value in enumerate(values[3:]):
                    W[n, c * zc + iz, pl.ds(8 * h, 8)] = value
            for (iz, h), values in zip(spots, tiles):
                for f in range(3):
                    if store:
                        packed[f] = put(q, c, f, iz, h, values[f], packed[f])
                    else:
                        out[f, c * zc + iz, pl.ds(8 * h, 8)] = values[f]
            return tuple(packed)

        packed = lax.fori_loop(0, zc // unroll, body, (zero, zero, zero))
        if store:
            for f in range(3):
                sy[q, c, f] = packed[f]

    for load in loads[2:6]:
        load.wait()

    def field_chunk(c, carry):
        def plane(iz, h):
            z, rows = c * zc + iz, pl.ds(8 * h, 8)
            kp = permeab[0, z, rows] * (1.0 - 0.95 * solid[0, z, rows].astype(f32))
            return kp, diffusivity[0, z, rows], conductivity[0, z, rows]

        chunk_of(0, c, plane, 8)
        send(0, c, False)
        return carry

    lax.fori_loop(0, CHUNKS, field_chunk, 0)

    for load in loads[:2] + loads[6:]:
        load.wait()
    tile = zero
    for h in range(2):
        rows = pl.ds(8 * h, 8)
        tile = tile + outlet[0, rows].astype(f32) * velocity[0, depth - 1, rows]
    part[0] = tile
    for d in range(1, ngx):
        flow_copy("gx", gx, ngx, d, part.at[0], got_x, True).start()

    for h in range(2):
        rows = pl.ds(8 * h, 8)
        keep[0, rows] = jnp.full((8, 128), 1.0 - OMEGA, f32)
        keep[1, rows] = (1.0 - OMEGA) * (1.0 - inlet[0, rows].astype(f32))
        extra[rows] = zero

    total = part[0]
    for d in range(1, ngx):
        flow_copy("gx", gx, ngx, d, part.at[0], got_x, True).wait_send()
        flow_copy("gx", gx, ngx, d, part.at[0], got_x, False).wait_recv()
        total = total + got_x[lax.rem(gx + ngx - d, ngx)]
    part[1] = total
    for d in range(1, ngy):
        flow_copy("gy", gy, ngy, d, part.at[1], got_y, True).start()

    def coef_chunk(c, carry):
        receive(0, c, False)
        cols = columns(0, c)

        def plane(iz, h):
            z, rows = c * zc + iz, pl.ds(8 * h, 8)
            bottom = (z == 0).astype(f32)
            top = (z == depth - 1).astype(f32)
            vel = velocity[0, z, rows]
            half = 0.5 * overpotential[0, z, rows]
            rate = 0.5 * (jnp.exp(half) + jnp.exp(-half))
            g = jnp.full((8, 128), MEMBRANE, f32) * bottom
            source = target[0, z, rows] + top * extra[rows]
            free = 1.0 - top * inlet[0, rows].astype(f32)
            rows_of = []
            for f in range(3):
                cen, near = around(0, c, f, iz, h, cols)
                w = [0.5 * (cen + k) for k in near]
                dsum = ((w[0] + w[1]) + (w[2] + w[3])) + (w[4] + w[5])
                if f == 0:
                    factor = OMEGA / (dsum + 1.0)
                    more = [factor * vel]
                elif f == 1:
                    factor = OMEGA * free / (dsum + vel + rate)
                    w[3] = w[3] + vel
                    start = factor * source
                    more = [start, factor * rate]
                else:
                    factor = OMEGA / (dsum + rate + g)
                    w[0] = w[0] * (1.0 - bottom) + g
                    more = [factor * rate]
                rows_of += [factor * k for k in w] + more
            return (zero, start, zero, *rows_of)

        chunk_of(1, c, plane, COEF_UNROLL)
        send(1, c, True)
        return carry

    lax.fori_loop(0, CHUNKS - 1, coef_chunk, 0)
    total = part[1]
    for d in range(1, ngy):
        flow_copy("gy", gy, ngy, d, part.at[1], got_y, True).wait_send()
        flow_copy("gy", gy, ngy, d, part.at[1], got_y, False).wait_recv()
        total = total + got_y[lax.rem(gy + ngy - d, ngy)]
    outflow = jnp.sum(jnp.sum(total, axis=0, keepdims=True), axis=1, keepdims=True)
    scale = jnp.broadcast_to((cells / 8.0) / (1.0 + outflow), (8, 128))
    for h in range(2):
        rows = pl.ds(8 * h, 8)
        extra[rows] = outlet[0, rows].astype(f32) * scale
    lax.fori_loop(CHUNKS - 1, CHUNKS, coef_chunk, 0)

    def sweep_chunk(p, q, c, final):
        receive(p, c, True)
        cols = columns(p, c)

        def plane(iz, h):
            z, rows = c * zc + iz, pl.ds(8 * h, 8)
            top = (z == depth - 1).astype(jnp.int32)

            def mixed(base, near):
                t = [W[base + n, z, rows] * near[n] for n in range(6)]
                return ((t[0] + t[1]) + (t[2] + t[3])) + (t[4] + t[5])

            pc, pn = around(p, c, 0, iz, h, cols)
            cc, cn = around(p, c, 1, iz, h, cols)
            ec, en = around(p, c, 2, iz, h, cols)
            p_new = mixed(0, pn) + ((1.0 - OMEGA) * pc + W[6, z, rows] * (cn[3] - cc))
            c_new = mixed(7, cn) + (keep[top, rows] * cc + (W[13, z, rows] + W[14, z, rows] * ec))
            e_new = mixed(15, en) + ((1.0 - OMEGA) * ec + W[21, z, rows] * cc)
            return p_new, c_new, e_new

        chunk_of(q, c, plane, UNROLL, not final)
        if not final:
            send(q, c, True)

    def sweep(t, carry):
        p = lax.rem(t, 2)

        def one(c, carry):
            sweep_chunk(p, 1 - p, c, False)
            return carry

        return lax.fori_loop(0, CHUNKS, one, carry)

    lax.fori_loop(1, ITERS - 1, sweep, 0)
    last = (ITERS - 1) % 2

    def store(c):
        span = pl.ds(c * zc, zc)
        return pltpu.make_async_copy(out.at[:, span], out_hbm.at[0, :, span], out_sem.at[c])

    def finish(c, carry):
        sweep_chunk(last, 1 - last, c, True)
        store(c).start()
        return carry

    def settle(c, carry):
        store(c).wait()
        return carry

    lax.fori_loop(0, CHUNKS, finish, 0)
    lax.fori_loop(0, CHUNKS, settle, 0)


def solution(mesh):
    ngx, ngy = mesh.shape["gx"], mesh.shape["gy"]

    def local(*args):
        depth = args[0].shape[1]
        zc = depth // CHUNKS
        hbm = pl.BlockSpec(memory_space=pl.ANY)
        return pl.pallas_call(
            functools.partial(kernel, ngx, ngy, depth),
            out_shape=jax.ShapeDtypeStruct((1, 3, depth, 16, 128), f32),
            in_specs=[hbm] * 9,
            out_specs=hbm,
            scratch_shapes=[pltpu.VMEM(a.shape, a.dtype) for a in args]
            + [
                pltpu.VMEM((3, depth, 16, 128), f32),
                pltpu.VMEM((2, 3, depth + 2, 32, 128), f32),
                pltpu.VMEM((22, depth, 16, 128), f32),
                pltpu.VMEM((2, 2, CHUNKS, 3, zc, 128), f32),
                pltpu.VMEM((2, 2, CHUNKS, 3, zc, 128), f32),
                pltpu.VMEM((2, CHUNKS, 3, 8, 128), f32),
                pltpu.VMEM((2, 2, CHUNKS, 3, 8, 128), f32),
                pltpu.VMEM((2, 16, 128), f32),
                pltpu.VMEM((16, 128), f32),
                pltpu.VMEM((2, 8, 128), f32),
                pltpu.VMEM((ngx, 8, 128), f32),
                pltpu.VMEM((ngy, 8, 128), f32),
                pltpu.SemaphoreType.DMA((2, 5, CHUNKS)),
                pltpu.SemaphoreType.DMA((2, 5, CHUNKS)),
                pltpu.SemaphoreType.DMA((2, max(ngx, ngy))),
                pltpu.SemaphoreType.DMA((2, max(ngx, ngy))),
                pltpu.SemaphoreType.DMA((9,)),
                pltpu.SemaphoreType.DMA((CHUNKS,)),
            ],
            compiler_params=pltpu.CompilerParams(
                collective_id=0, has_side_effects=True, vmem_limit_bytes=48 * 1024 * 1024
            ),
        )(*args)

    placed = (
        (P("side", None, "gx", "gy"),) * 6
        + (P("side", "gx", "gy"),) * 2
        + (P(("groups", "side"), None, "gx", "gy"),)
    )
    return jax.shard_map(
        local,
        mesh=mesh,
        in_specs=placed,
        out_specs=P(("groups", "side"), None, None, "gx", "gy"),
        check_vma=False,
    )
```
